32 devices in a mesh: row: 8 (over y, x, core), col: 4 (over z).
Axes of the slice: x: 2, y: 2, z: 4, core: 2. Of those that a mesh axis runs over, the one named last changes fastest.
Arguments:
- screen: int32 [1536, 3], P(('row', 'col')), may hold values from 0 to 31, as said below
- values: bfloat16 [1536, 128, 128], P(('row', 'col')), may hold values from -6 to 6
- sizes: int32 [32], replicated, may hold values from 64 to 128
- slot: int32 [32], replicated, may hold values from 0 to 31, as said below
- orbitals: bfloat16 [4096, 512], P('col'), may hold values from -0.15625 to 0.15625
Outputs:
- half_transformed: bfloat16 [4096, 4, 512], P(('row', 'col'))
The draws below stay inside these ranges and needn't reach their ends.
Inputs may be any that keep to these rules, and one draw needn't show every extreme that they name: `screen`: columns hold a, b, q with a and b below 32 and q below 4. The rows of device d (rows d * 48 onward, devices in row-major order) name blocks b in column group d % 4, that is b // 8 equals it. Among one device's rows at most 6 have slot[a] // 4 equal to any one value, and on every device some value is taken by exactly 6 rows. Triples may repeat. `slot`: A permutation of the block numbers.
All inputs are finite; a program needn't handle non-finite values.
Results may differ from the reference program's by a relative error of at most 0.0015.
Values may be sent and summed in bfloat16 or wider, within the bound.
A program may use at most 64 MiB of HBM per device.

```python
import math
import jax
import jax.numpy as jnp
from jax import lax

BS = 128
BLK_DEV = 4
NNZ_DEV = 48
NQ = 4
NOCC = 512
NB = 32
NBAS = 4096
NNZ = 1536
CAP = 6
N_ROW = 8
N_COL = 4


def block_order(key):
    return jax.random.permutation(key, NB).astype(jnp.int32)


def draw_slot(key, part):
    order = block_order(key)
    return jnp.zeros((NB,), jnp.int32).at[order].set(jnp.arange(NB, dtype=jnp.int32))


def draw_screen(key, part):
    order = block_order(key)
    key = jax.random.fold_in(key, 5)
    key_hot, key_perm, key_inner, key_cols, key_ri = jax.random.split(key, 5)
    device_total = NNZ // NNZ_DEV
    rows = jnp.arange(NNZ, dtype=jnp.int32)
    device = rows // NNZ_DEV
    within = rows % NNZ_DEV
    column = device % N_COL
    pick = jax.random.randint(key_hot, (device_total,), 0, N_ROW).astype(jnp.int32)
    hottest = pick * pick // N_ROW
    perm_keys = jax.random.split(key_perm, device_total)
    others = jax.vmap(lambda k: jax.random.permutation(k, N_ROW - 1))(perm_keys).astype(jnp.int32)
    spread = others[device, (within - CAP) % (N_ROW - 1)]
    target = jnp.where(within < CAP, hottest[device], (hottest[device] + 1 + spread) % N_ROW)
    inner = jax.random.randint(key_inner, (NNZ,), 0, BLK_DEV).astype(jnp.int32)
    first = order[target * BLK_DEV + inner]
    per_col = NB // N_COL
    second = column * per_col + jax.random.randint(key_cols, (NNZ,), 0, per_col).astype(jnp.int32)
    ri_func = jax.random.randint(key_ri, (NNZ,), 0, NQ).astype(jnp.int32)
    return jnp.stack([first, second, ri_func], axis=1)


def place_ends(values, key, least, top_value):
    shape = values.shape
    place = [jax.random.randint(jax.random.fold_in(key, axis), (), 0, shape[axis]) for axis in range(len(shape))]
    values = values.at[tuple(place)].set(least)
    longest = shape.index(max(shape))
    place[longest] = (place[longest] + 1) % shape[longest]
    return values.at[tuple(place)].set(top_value)


def shard_levels(key, shape, pieces, smallest, high):
    level = 1.0
    for axis_at, blocks in pieces:
        draws = jax.random.uniform(jax.random.fold_in(jax.random.fold_in(key, 6), axis_at), (blocks,), jnp.float32, smallest / len(pieces), high / len(pieces))
        level = level * jnp.repeat(jnp.exp(draws), shape[axis_at] // blocks).reshape((-1,) + (1,) * (len(shape) - 1 - axis_at))
    return level


def normal_values(rng, dims, scale, bound, pieces=(), kind=jnp.bfloat16):
    entries = scale * jax.random.normal(rng, dims, jnp.float32)
    if pieces:
        entries = entries * shard_levels(rng, dims, pieces, -0.22, 0.18)
    return jnp.clip(entries, -bound, bound).astype(kind)


def setup_inputs(seed: int = 0) -> dict:
    key_of = jax.random.split(jax.random.key(seed), 6)
    return {
        "screen": draw_screen(jax.random.fold_in(key_of[5], 71), 0),
        "values": normal_values(key_of[1], (NNZ, BS, BS), 1.0, 6.0, ((0, 32),)),
        "sizes": place_ends(jax.random.randint(key_of[2], (NB,), BS // 2, BS + 1), jax.random.fold_in(key_of[2], 1), BS // 2, BS).astype(jnp.int32),
        "slot": draw_slot(jax.random.fold_in(key_of[5], 71), 0),
        "orbitals": normal_values(key_of[4], (NBAS, NOCC), (NNZ_DEV * N_COL * BS // (NQ * BLK_DEV)) ** -0.5, 0.15625, ((0, 4),)),
    }


def reference(screen, values, sizes, slot, orbitals):
    keep = (jnp.arange(BS)[None, :] < sizes[:, None]).astype(orbitals.dtype)
    coeffs = orbitals.reshape(NB, BS, NOCC) * keep[:, :, None]
    group = math.gcd(NNZ, 256)
    rounds = NNZ // group
    placed = slot[screen[:, 0]].astype(jnp.int32)

    def accumulate(totals, batch):
        block_vals, block_b, block_q, block_slot = batch
        picked = coeffs[block_b].astype(jnp.float32)
        product = jnp.einsum("gmn,gno->gmo", block_vals.astype(jnp.float32), picked,
                             precision=lax.Precision.HIGHEST)
        totals = totals.at[block_slot, :, block_q, :].add(product)
        return totals, None

    start = jnp.zeros((NB, BS, NQ, NOCC), jnp.float32)
    totals, unused = lax.scan(accumulate, start, (
        values.reshape(rounds, group, BS, BS),
        screen[:, 1].reshape(rounds, group),
        screen[:, 2].reshape(rounds, group),
        placed.reshape(rounds, group)))
    inverse = jnp.zeros((NB,), jnp.int32).at[slot].set(jnp.arange(NB, dtype=jnp.int32))
    slot_sizes = sizes[inverse]
    live = (jnp.arange(BS)[None, :] < slot_sizes[:, None]).astype(jnp.float32)
    result = totals * live[:, :, None, None]
    return result.reshape(NBAS, NQ, NOCC).astype(jnp.bfloat16)
```

```python
import functools

import jax
import jax.numpy as jnp
from jax import lax
from jax.experimental import pallas as pl
from jax.experimental.pallas import tpu as pltpu
from jax.sharding import PartitionSpec as P

NQ = 4
LANES = 128
VMEM_LIMIT = 48 * 1024 * 1024


def order_kernel(rows, capacity, per_row, per_col, screen_ref, slot_ref, order_ref, label_ref, count):
    listed = screen_ref.shape[0]

    @pl.loop(0, rows)
    def clear(r):
        count[r] = 0

    @pl.loop(0, rows * capacity)
    def empty(k):
        order_ref[k] = 0
        label_ref[k] = -1

    @pl.loop(0, listed)
    def place(k):
        placed = slot_ref[screen_ref[k, 0]]
        owner = placed // per_row
        seat = owner * capacity + count[owner]
        count[owner] = count[owner] + 1
        order_ref[seat] = k
        out_block = (placed % per_row) * NQ + screen_ref[k, 2]
        label_ref[seat] = out_block * per_col + screen_ref[k, 1] % per_col


def exchange_kernel(
    rows, capacity, order_ref, label_ref, values_ref, got_ref, got_label_ref,
    send, send_label, send_sem, recv_sem, send_label_sem, recv_label_sem,
):
    me = lax.axis_index("row")
    barrier = pltpu.get_barrier_semaphore()
    for step in range(1, rows):
        pl.semaphore_signal(
            barrier, inc=1, device_id={"row": lax.rem(me + step, rows)},
            device_id_type=pl.DeviceIdType.MESH,
        )
    lane = lax.broadcasted_iota(jnp.int32, (1, LANES), 1)

    def fill_label(row):
        line = jnp.full((1, LANES), -1, jnp.int32)
        for j in range(capacity):
            line = jnp.where(lane == j, label_ref[row * capacity + j], line)
        return line

    def copies(step):
        target = lax.rem(me + step, rows)
        return (
            pltpu.make_async_remote_copy(
                src_ref=send.at[step - 1],
                dst_ref=got_ref.at[pl.ds(step * capacity, capacity)],
                send_sem=send_sem.at[step - 1],
                recv_sem=recv_sem.at[step - 1],
                device_id={"row": target},
                device_id_type=pl.DeviceIdType.MESH,
            ),
            pltpu.make_async_remote_copy(
                src_ref=send_label.at[step - 1],
                dst_ref=got_label_ref.at[step],
                send_sem=send_label_sem.at[step - 1],
                recv_sem=recv_label_sem.at[step - 1],
                device_id={"row": target},
                device_id_type=pl.DeviceIdType.MESH,
            ),
        )

    pl.semaphore_wait(barrier, rows - 1)
    for step in range(1, rows):
        target = lax.rem(me + step, rows)
        for j in range(capacity):
            send[step - 1, j] = values_ref[order_ref[target * capacity + j]]
        send_label[step - 1] = fill_label(target)
        for copy in copies(step):
            copy.start()
    for j in range(capacity):
        got_ref[j] = values_ref[order_ref[me * capacity + j]]
    got_label_ref[0] = fill_label(me)
    for step in range(1, rows):
        for copy in copies(step):
            copy.wait()


def contract_kernel(
    capacity, per_col, label_ref, sizes_ref, got_ref, orbitals_ref,
    packed_ref, unit_ref, own_ref, totals, coeffs,
):
    width = got_ref.shape[1]
    cols, nq, rows_out, _ = packed_ref.shape
    splits = width // rows_out
    col = lax.axis_index("col")
    vertical = lax.broadcasted_iota(jnp.int32, (width, 1), 0)
    for b in range(per_col):
        size = sizes_ref[col * per_col + b]
        block = orbitals_ref[pl.ds(b * width, width), :].astype(jnp.float32)
        coeffs[b] = jnp.where(vertical < size, block, 0.0).astype(coeffs.dtype)

    @pl.loop(0, totals.shape[0])
    def clear(t):
        totals[t] = jnp.zeros(totals.shape[1:], jnp.float32)

    @pl.loop(0, got_ref.shape[0])
    def add(k):
        label = label_ref[k // capacity, 0, k % capacity]

        @pl.when(label >= 0)
        def listed():
            totals[label // per_col] += jnp.dot(
                got_ref[k], coeffs[label % per_col], preferred_element_type=jnp.float32
            )

    def tile(c, q):
        return totals[
            (c // splits) * nq + q, pl.ds(pl.multiple_of((c % splits) * rows_out, rows_out), rows_out)
        ]

    @pl.loop(0, cols * nq)
    def code(t):
        c, q = t // nq, t % nq
        part = tile(c, q)
        top = jnp.max(jnp.max(jnp.abs(part), axis=0, keepdims=True), axis=1, keepdims=True)
        unit = jnp.maximum(top, 1e-30) * 2.0**-15
        unit_ref[c, q] = jnp.broadcast_to(unit, (8, LANES))
        scaled = part * (1.0 / unit)
        power = scaled * scaled
        power = power * power
        power = power * power
        packed_ref[c, q] = jnp.where(scaled < 0.0, -power, power).astype(packed_ref.dtype)

    for q in range(nq):
        own_ref[q] = tile(col, q)


def scatter_kernel(
    cols, blocks_all, width, slot_ref, sizes_ref, packed_ref, unit_ref, own_ref, out_ref,
    got, got_unit, total, send_sem, recv_sem, send_unit_sem, recv_unit_sem,
):
    me = lax.axis_index("col")
    nq, rows_out, _ = own_ref.shape
    barrier = pltpu.get_barrier_semaphore()
    for step in range(1, cols):
        pl.semaphore_signal(
            barrier, inc=1, device_id={"col": lax.rem(me + step, cols)},
            device_id_type=pl.DeviceIdType.MESH,
        )
    pl.semaphore_wait(barrier, cols - 1)

    def unit_copy(step):
        target = lax.rem(me + step, cols)
        return pltpu.make_async_remote_copy(
            src_ref=unit_ref.at[target],
            dst_ref=got_unit.at[step - 1],
            send_sem=send_unit_sem.at[step - 1],
            recv_sem=recv_unit_sem.at[step - 1],
            device_id={"col": target},
            device_id_type=pl.DeviceIdType.MESH,
        )

    def part_copy(step, q):
        target = lax.rem(me + step, cols)
        return pltpu.make_async_remote_copy(
            src_ref=packed_ref.at[target, q],
            dst_ref=got.at[step - 1, q],
            send_sem=send_sem.at[step - 1, q],
            recv_sem=recv_sem.at[step - 1, q],
            device_id={"col": target},
            device_id_type=pl.DeviceIdType.MESH,
        )

    for step in range(1, cols):
        unit_copy(step).start()
    for q in range(nq):
        for step in range(1, cols):
            part_copy(step, q).start()

    first_row = (lax.axis_index("row") * cols + me) * rows_out
    mine = first_row // width
    size = jnp.int32(0)
    for b in range(blocks_all):
        size = jnp.where(slot_ref[b] == mine, sizes_ref[b], size)
    vertical = lax.broadcasted_iota(jnp.int32, (rows_out, 1), 0) + lax.rem(first_row, width)
    live = vertical < size

    for step in range(1, cols):
        unit_copy(step).wait()
    for q in range(nq):
        for step in range(1, cols):
            part_copy(step, q).wait()
            coded = got[step - 1, q].astype(jnp.float32)
            root = jnp.exp(0.125 * jnp.log(jnp.abs(coded)))
            root = jnp.where(coded < 0.0, -root, jnp.where(coded > 0.0, root, 0.0))
            before = own_ref[q] if step == 1 else total[...]
            total[...] = before + root * got_unit[step - 1, q, 0:1, 0:1]
        out_ref[q] = jnp.where(live, total[...], 0.0).astype(out_ref.dtype)


def on_device(screen, values, sizes, slot, orbitals):
    rows = lax.axis_size("row")
    cols = lax.axis_size("col")
    blocks_all = sizes.shape[0]
    listed, width = values.shape[:2]
    orbital_count = orbitals.shape[1]
    per_row = blocks_all // rows
    per_col = blocks_all // cols
    capacity = max(4, -(-listed // rows))
    seats = rows * capacity
    smem = pl.BlockSpec(memory_space=pltpu.SMEM)
    vmem = pl.BlockSpec(memory_space=pltpu.VMEM)
    dma = pltpu.SemaphoreType.DMA

    order, labels = pl.pallas_call(
        functools.partial(order_kernel, rows, capacity, per_row, per_col),
        out_shape=[jax.ShapeDtypeStruct((seats,), jnp.int32)] * 2,
        in_specs=[smem] * 2,
        out_specs=[smem] * 2,
        scratch_shapes=[pltpu.SMEM((rows,), jnp.int32)],
        name="order_blocks",
    )(screen, slot)

    got, got_labels = pl.pallas_call(
        functools.partial(exchange_kernel, rows, capacity),
        out_shape=[
            jax.ShapeDtypeStruct((seats, width, width), values.dtype),
            jax.ShapeDtypeStruct((rows, 1, LANES), jnp.int32),
        ],
        in_specs=[smem, smem, vmem],
        out_specs=[vmem] * 2,
        scratch_shapes=[
            pltpu.VMEM((rows - 1, capacity, width, width), values.dtype),
            pltpu.VMEM((rows - 1, 1, LANES), jnp.int32),
            dma((rows - 1,)), dma((rows - 1,)), dma((rows - 1,)), dma((rows - 1,)),
        ],
        compiler_params=pltpu.CompilerParams(
            collective_id=0, has_side_effects=True, vmem_limit_bytes=VMEM_LIMIT
        ),
        name="exchange_blocks",
    )(order, labels, values)

    rows_out = per_row * width // cols
    packed, units, own = pl.pallas_call(
        functools.partial(contract_kernel, capacity, per_col),
        out_shape=[
            jax.ShapeDtypeStruct((cols, NQ, rows_out, orbital_count), jnp.bfloat16),
            jax.ShapeDtypeStruct((cols, NQ, 8, LANES), jnp.float32),
            jax.ShapeDtypeStruct((NQ, rows_out, orbital_count), jnp.float32),
        ],
        in_specs=[smem, smem, vmem, vmem],
        out_specs=[vmem] * 3,
        scratch_shapes=[
            pltpu.VMEM((per_row * NQ, width, orbital_count), jnp.float32),
            pltpu.VMEM((per_col, width, orbital_count), orbitals.dtype),
        ],
        compiler_params=pltpu.CompilerParams(vmem_limit_bytes=VMEM_LIMIT),
        name="contract_blocks",
    )(got_labels, sizes, got, orbitals)

    summed = pl.pallas_call(
        functools.partial(scatter_kernel, cols, blocks_all, width),
        out_shape=jax.ShapeDtypeStruct((NQ, rows_out, orbital_count), jnp.bfloat16),
        in_specs=[smem, smem, vmem, vmem, vmem],
        out_specs=vmem,
        scratch_shapes=[
            pltpu.VMEM((cols - 1, NQ, rows_out, orbital_count), jnp.bfloat16),
            pltpu.VMEM((cols - 1, NQ, 8, LANES), jnp.float32),
            pltpu.VMEM((rows_out, orbital_count), jnp.float32),
            dma((cols - 1, NQ)), dma((cols - 1, NQ)), dma((cols - 1,)), dma((cols - 1,)),
        ],
        compiler_params=pltpu.CompilerParams(
            collective_id=1, has_side_effects=True, vmem_limit_bytes=VMEM_LIMIT
        ),
        name="scatter_sums",
    )(slot, sizes, packed, units, own)
    return summed.transpose(1, 0, 2)


def solution(mesh):
    in_specs = (P(("row", "col"), None), P(("row", "col"), None, None), P(), P(), P("col", None))
    out_specs = P(("row", "col"), None, None)
    return jax.shard_map(
        on_device, mesh=mesh, in_specs=in_specs, out_specs=out_specs, check_vma=False
    )
```

```python
import functools

import jax
import jax.numpy as jnp
from jax import lax
from jax.experimental import pallas as pl
from jax.experimental.pallas import tpu as pltpu
from jax.sharding import PartitionSpec as P

NQ = 4
LANES = 128
LAG = 2
VMEM_LIMIT = 20 * 1024 * 1024


def order_kernel(rows, capacity, per_row, per_col, screen_ref, slot_ref, order_ref, label_ref, count):
    listed = screen_ref.shape[0]

    @pl.loop(0, rows)
    def clear(r):
        count[r] = 0

    @pl.loop(0, rows * capacity, unroll=8)
    def empty(k):
        order_ref[k] = 0
        label_ref[k] = -1

    @pl.loop(0, listed, unroll=8)
    def place(k):
        placed = slot_ref[screen_ref[k, 0]]
        owner = placed // per_row
        seat = owner * capacity + count[owner]
        count[owner] = count[owner] + 1
        order_ref[seat] = k
        out_block = (placed % per_row) * NQ + screen_ref[k, 2]
        label_ref[seat] = out_block * per_col + screen_ref[k, 1] % per_col


def exchange_kernel(
    rows, capacity, order_ref, label_ref, values_ref, got_ref, got_label_ref,
    send, send_label, send_sem, recv_sem, send_label_sem, recv_label_sem,
):
    me = lax.axis_index("row")
    barrier = pltpu.get_barrier_semaphore()
    for step in range(1, rows):
        pl.semaphore_signal(
            barrier, inc=1, device_id={"row": lax.rem(me + step, rows)},
            device_id_type=pl.DeviceIdType.MESH,
        )
    lane = lax.broadcasted_iota(jnp.int32, (1, LANES), 1)

    def fill_label(row):
        line = jnp.full((1, LANES), -1, jnp.int32)
        for j in range(capacity):
            line = jnp.where(lane == j, label_ref[row * capacity + j], line)
        return line

    def copies(step):
        target = lax.rem(me + step, rows)
        return (
            pltpu.make_async_remote_copy(
                src_ref=send.at[step - 1],
                dst_ref=got_ref.at[pl.ds(step * capacity, capacity)],
                send_sem=send_sem.at[step - 1],
                recv_sem=recv_sem.at[step - 1],
                device_id={"row": target},
                device_id_type=pl.DeviceIdType.MESH,
            ),
            pltpu.make_async_remote_copy(
                src_ref=send_label.at[step - 1],
                dst_ref=got_label_ref.at[step],
                send_sem=send_label_sem.at[step - 1],
                recv_sem=recv_label_sem.at[step - 1],
                device_id={"row": target},
                device_id_type=pl.DeviceIdType.MESH,
            ),
        )

    pl.semaphore_wait(barrier, rows - 1)
    for step in range(1, rows):
        target = lax.rem(me + step, rows)
        for j in range(capacity):
            send[step - 1, j] = values_ref[order_ref[target * capacity + j]]
        send_label[step - 1] = fill_label(target)
        for copy in copies(step):
            copy.start()
    for j in range(capacity):
        got_ref[j] = values_ref[order_ref[me * capacity + j]]
    got_label_ref[0] = fill_label(me)
    for step in range(1, rows):
        for copy in copies(step):
            copy.wait()


def contract_kernel(
    capacity, per_col, label_ref, sizes_ref, got_ref, orbitals_ref, totals_ref, coeffs
):
    width = got_ref.shape[1]
    col = lax.axis_index("col")
    vertical = lax.broadcasted_iota(jnp.int32, (width, 1), 0)
    for b in range(per_col):
        size = sizes_ref[col * per_col + b]
        block = orbitals_ref[pl.ds(b * width, width), :].astype(jnp.float32)
        coeffs[b] = jnp.where(vertical < size, block, 0.0).astype(coeffs.dtype)

    @pl.loop(0, totals_ref.shape[0])
    def clear(t):
        totals_ref[t] = jnp.zeros(totals_ref.shape[1:], jnp.float32)

    @pl.loop(0, got_ref.shape[0], unroll=2)
    def add(k):
        label = label_ref[k // capacity, 0, k % capacity]

        @pl.when(label >= 0)
        def listed():
            totals_ref[label // per_col] += jnp.dot(
                got_ref[k], coeffs[label % per_col], preferred_element_type=jnp.float32
            )


def scatter_kernel(
    cols, blocks_all, slot_ref, sizes_ref, totals_ref, out_ref, send, got, total, send_sem, recv_sem
):
    me = lax.axis_index("col")
    nq, rows_out, orbital_count = out_ref.shape
    width = totals_ref.shape[1]
    splits = width // rows_out
    sides = (me > 0, me < cols - 1)
    barrier = pltpu.get_barrier_semaphore()
    for step in range(1, cols):
        pl.semaphore_signal(
            barrier, inc=1, device_id={"col": lax.rem(me + step, cols)},
            device_id_type=pl.DeviceIdType.MESH,
        )
    pl.semaphore_wait(barrier, cols - 1)

    def copy(up, target, q):
        return pltpu.make_async_remote_copy(
            src_ref=send.at[target, q],
            dst_ref=got.at[up, target, q],
            send_sem=send_sem.at[target, q],
            recv_sem=recv_sem.at[up, target, q],
            device_id={"col": me + 1 if up else me - 1},
            device_id_type=pl.DeviceIdType.MESH,
        )

    strip = min(rows_out, 32)

    def own(c, q, at):
        first = pl.multiple_of((c % splits) * rows_out + at, strip)
        return totals_ref[(c // splits) * nq + q, pl.ds(first, strip)]

    def decode(up, c, q, at, unit):
        coded = got[up, c, q, pl.ds(at, strip), :].astype(jnp.float32)
        root = jnp.exp2(0.125 * jnp.log2(jnp.abs(coded)))
        return jnp.where(coded < 0.0, -root, root) * unit

    def unit_of(up, c, q):
        return got[up, c, q, pl.ds(rows_out, 16), :].astype(jnp.float32)[0:1, :]

    def code(c, q, parts):
        top = jnp.zeros((8, orbital_count), jnp.float32)
        for at in range(0, rows_out, strip):
            part = parts(at)
            total[pl.ds(at, strip), :] = part
            top = jnp.maximum(top, jnp.max(jnp.abs(part).reshape(-1, 8, orbital_count), axis=0))
        top = jnp.max(jnp.max(top, axis=0, keepdims=True), axis=1, keepdims=True)
        unit = (jnp.maximum(top, 1e-30) * (1.01 * 2.0**-15)).astype(send.dtype)
        send[c, q, pl.ds(rows_out, 16), :] = jnp.broadcast_to(unit, (16, orbital_count))
        inverse = 1.0 / unit.astype(jnp.float32)
        for at in range(0, rows_out, strip):
            scaled = total[pl.ds(at, strip), :] * inverse
            power = scaled * scaled
            power = power * power
            power = power * power
            send[c, q, pl.ds(at, strip), :] = jnp.where(scaled < 0.0, -power, power).astype(send.dtype)

    @pl.loop(0, (cols - 1) * nq)
    def ends(k):
        i, q = k // nq, k % nq
        for up, target, end in ((1, cols - 1 - i, 0), (0, i, cols - 1)):
            @pl.when(me == end)
            def begin():
                code(target, q, lambda at: own(target, q, at))
                copy(up, target, q).start()

    tiles = (cols - 1) * nq

    @pl.loop(0, tiles + (cols - 1) * LAG)
    def between(k):
        for up in (1, 0):
            turn = k - LAG * (me if up else cols - 1 - me)
            i, q = turn // nq, turn % nq
            target = cols - 1 - i if up else i
            inside = (me > 0) & (me < target) if up else (me < cols - 1) & (me > target)

            @pl.when((turn >= 0) & (turn < tiles) & inside)
            def forward():
                copy(up, target, q).wait_recv()
                unit = unit_of(up, target, q)
                code(target, q, lambda at: own(target, q, at) + decode(up, target, q, at, unit))
                copy(up, target, q).start()

    first_row = (lax.axis_index("row") * cols + me) * rows_out
    mine = first_row // width
    size = jnp.int32(0)
    for b in range(blocks_all):
        size = jnp.where(slot_ref[b] == mine, sizes_ref[b], size)
    vertical = lax.broadcasted_iota(jnp.int32, (strip, 1), 0) + lax.rem(first_row, width)

    total[...] = jnp.zeros(total.shape, jnp.float32)

    @pl.loop(0, nq)
    def finish(q):
        for up, side in ((1, sides[0]), (0, sides[1])):
            @pl.when(side)
            def arrived():
                copy(up, me, q).wait_recv()
                unit = unit_of(up, me, q)
                for at in range(0, rows_out, strip):
                    if up:
                        before = own(me, q, at)
                    else:
                        before = jnp.where(sides[0], total[pl.ds(at, strip), :], own(me, q, at))
                    total[pl.ds(at, strip), :] = before + decode(up, me, q, at, unit)
        for at in range(0, rows_out, strip):
            kept = jnp.where(vertical + at < size, total[pl.ds(at, strip), :], 0.0)
            out_ref[q, pl.ds(at, strip), :] = kept.astype(out_ref.dtype)

    @pl.loop(0, cols * nq)
    def drain(k):
        @pl.when(me != k // nq)
        def sent():
            copy(1, k // nq, k % nq).wait_send()


def on_device(screen, values, sizes, slot, orbitals):
    rows = lax.axis_size("row")
    cols = lax.axis_size("col")
    blocks_all = sizes.shape[0]
    listed, width = values.shape[:2]
    orbital_count = orbitals.shape[1]
    per_row = blocks_all // rows
    per_col = blocks_all // cols
    capacity = max(4, -(-listed // rows))
    seats = rows * capacity
    smem = pl.BlockSpec(memory_space=pltpu.SMEM)
    vmem = pl.BlockSpec(memory_space=pltpu.VMEM)
    dma = pltpu.SemaphoreType.DMA

    order, labels = pl.pallas_call(
        functools.partial(order_kernel, rows, capacity, per_row, per_col),
        out_shape=[jax.ShapeDtypeStruct((seats,), jnp.int32)] * 2,
        in_specs=[smem] * 2,
        out_specs=[smem] * 2,
        scratch_shapes=[pltpu.SMEM((rows,), jnp.int32)],
        name="order_blocks",
    )(screen, slot)

    got, got_labels = pl.pallas_call(
        functools.partial(exchange_kernel, rows, capacity),
        out_shape=[
            jax.ShapeDtypeStruct((seats, width, width), values.dtype),
            jax.ShapeDtypeStruct((rows, 1, LANES), jnp.int32),
        ],
        in_specs=[smem, smem, vmem],
        out_specs=[vmem] * 2,
        scratch_shapes=[
            pltpu.VMEM((rows - 1, capacity, width, width), values.dtype),
            pltpu.VMEM((rows - 1, 1, LANES), jnp.int32),
            dma((rows - 1,)), dma((rows - 1,)), dma((rows - 1,)), dma((rows - 1,)),
        ],
        compiler_params=pltpu.CompilerParams(
            collective_id=0, has_side_effects=True, vmem_limit_bytes=VMEM_LIMIT
        ),
        name="exchange_blocks",
    )(order, labels, values)

    rows_out = per_row * width // cols
    totals = pl.pallas_call(
        functools.partial(contract_kernel, capacity, per_col),
        out_shape=jax.ShapeDtypeStruct((per_row * NQ, width, orbital_count), jnp.float32),
        in_specs=[smem, smem, vmem, vmem],
        out_specs=vmem,
        scratch_shapes=[pltpu.VMEM((per_col, width, orbital_count), orbitals.dtype)],
        compiler_params=pltpu.CompilerParams(vmem_limit_bytes=VMEM_LIMIT),
        name="contract_blocks",
    )(got_labels, sizes, got, orbitals)

    summed = pl.pallas_call(
        functools.partial(scatter_kernel, cols, blocks_all),
        out_shape=jax.ShapeDtypeStruct((NQ, rows_out, orbital_count), jnp.bfloat16),
        in_specs=[smem, smem, vmem],
        out_specs=vmem,
        scratch_shapes=[
            pltpu.VMEM((cols, NQ, rows_out + 16, orbital_count), jnp.bfloat16),
            pltpu.VMEM((2, cols, NQ, rows_out + 16, orbital_count), jnp.bfloat16),
            pltpu.VMEM((rows_out, orbital_count), jnp.float32),
            dma((cols, NQ)), dma((2, cols, NQ)),
        ],
        compiler_params=pltpu.CompilerParams(
            collective_id=1, has_side_effects=True, vmem_limit_bytes=VMEM_LIMIT
        ),
        name="scatter_sums",
    )(slot, sizes, totals)
    return summed.transpose(1, 0, 2)


def solution(mesh):
    in_specs = (P(("row", "col"), None), P(("row", "col"), None, None), P(), P(), P("col", None))
    out_specs = P(("row", "col"), None, None)
    return jax.shard_map(
        on_device, mesh=mesh, in_specs=in_specs, out_specs=out_specs, check_vma=False
    )
```

```python
import functools

import jax
import jax.numpy as jnp
from jax import lax
from jax.experimental import pallas as pl
from jax.experimental.pallas import tpu as pltpu
from jax.sharding import PartitionSpec as P

NQ = 4
LANES = 128
LAG = 2
VMEM_LIMIT = 20 * 1024 * 1024


def order_kernel(rows, capacity, per_row, per_col, screen_ref, slot_ref, order_ref, label_ref, count):
    listed = screen_ref.shape[0]

    @pl.loop(0, rows)
    def clear(r):
        count[r] = 0

    @pl.loop(0, rows * capacity, unroll=8)
    def empty(k):
        order_ref[k] = 0
        label_ref[k] = -1

    @pl.loop(0, listed, unroll=8)
    def place(k):
        placed = slot_ref[screen_ref[k, 0]]
        owner = placed // per_row
        seat = owner * capacity + count[owner]
        count[owner] = count[owner] + 1
        order_ref[seat] = k
        out_block = (placed % per_row) * NQ + screen_ref[k, 2]
        label_ref[seat] = out_block * per_col + screen_ref[k, 1] % per_col


def exchange_kernel(
    rows, capacity, order_ref, label_ref, values_ref, got_ref, got_label_ref,
    send, send_label, send_sem, recv_sem, send_label_sem, recv_label_sem,
):
    me = lax.axis_index("row")
    barrier = pltpu.get_barrier_semaphore()
    for step in range(1, rows):
        pl.semaphore_signal(
            barrier, inc=1, device_id={"row": lax.rem(me + step, rows)},
            device_id_type=pl.DeviceIdType.MESH,
        )
    lane = lax.broadcasted_iota(jnp.int32, (1, LANES), 1)

    def fill_label(row):
        line = jnp.full((1, LANES), -1, jnp.int32)
        for j in range(capacity):
            line = jnp.where(lane == j, label_ref[row * capacity + j], line)
        return line

    def copies(step):
        target = lax.rem(me + step, rows)
        return (
            pltpu.make_async_remote_copy(
                src_ref=send.at[step - 1],
                dst_ref=got_ref.at[pl.ds(step * capacity, capacity)],
                send_sem=send_sem.at[step - 1],
                recv_sem=recv_sem.at[step - 1],
                device_id={"row": target},
                device_id_type=pl.DeviceIdType.MESH,
            ),
            pltpu.make_async_remote_copy(
                src_ref=send_label.at[step - 1],
                dst_ref=got_label_ref.at[step],
                send_sem=send_label_sem.at[step - 1],
                recv_sem=recv_label_sem.at[step - 1],
                device_id={"row": target},
                device_id_type=pl.DeviceIdType.MESH,
            ),
        )

    pl.semaphore_wait(barrier, rows - 1)
    for step in range(1, rows):
        target = lax.rem(me + step, rows)
        for j in range(capacity):
            send[step - 1, j] = values_ref[order_ref[target * capacity + j]]
        send_label[step - 1] = fill_label(target)
        for copy in copies(step):
            copy.start()
    for j in range(capacity):
        got_ref[j] = values_ref[order_ref[me * capacity + j]]
    got_label_ref[0] = fill_label(me)
    for step in range(1, rows):
        for copy in copies(step):
            copy.wait()


def contract_kernel(
    capacity, per_col, label_ref, sizes_ref, got_ref, orbitals_ref, totals_ref, coeffs
):
    width = got_ref.shape[1]
    col = lax.axis_index("col")
    vertical = lax.broadcasted_iota(jnp.int32, (width, 1), 0)
    for b in range(per_col):
        size = sizes_ref[col * per_col + b]
        block = orbitals_ref[pl.ds(b * width, width), :].astype(jnp.float32)
        coeffs[b] = jnp.where(vertical < size, block, 0.0).astype(coeffs.dtype)

    @pl.loop(0, totals_ref.shape[0])
    def clear(t):
        totals_ref[t] = jnp.zeros(totals_ref.shape[1:], jnp.float32)

    group = 4

    @pl.loop(0, got_ref.shape[0] // group)
    def add(g):
        places = [g * group + j for j in range(group)]
        labels = [label_ref[k // capacity, 0, k % capacity] for k in places]
        products = [
            jnp.dot(
                got_ref[k], coeffs[jnp.maximum(label, 0) % per_col],
                preferred_element_type=jnp.float32,
            )
            for k, label in zip(places, labels)
        ]
        for label, product in zip(labels, products):
            @pl.when(label >= 0)
            def listed():
                totals_ref[label // per_col] += product


def scatter_kernel(
    cols, blocks_all, slot_ref, sizes_ref, totals_ref, out_ref, send, got, send_unit, got_unit, total,
    send_sem, recv_sem, send_unit_sem, recv_unit_sem,
):
    me = lax.axis_index("col")
    nq, rows_out, orbital_count = out_ref.shape
    width = totals_ref.shape[1]
    splits = width // rows_out
    sides = (me > 0, me < cols - 1)
    barrier = pltpu.get_barrier_semaphore()
    for step in range(1, cols):
        pl.semaphore_signal(
            barrier, inc=1, device_id={"col": lax.rem(me + step, cols)},
            device_id_type=pl.DeviceIdType.MESH,
        )
    pl.semaphore_wait(barrier, cols - 1)

    class Pair:
        def __init__(self, up, target, q):
            where = dict(
                device_id={"col": me + 1 if up else me - 1}, device_id_type=pl.DeviceIdType.MESH
            )
            self.both = (
                pltpu.make_async_remote_copy(
                    src_ref=send_unit.at[target, q],
                    dst_ref=got_unit.at[up, target, q],
                    send_sem=send_unit_sem.at[target, q],
                    recv_sem=recv_unit_sem.at[up, target, q],
                    **where,
                ),
                pltpu.make_async_remote_copy(
                    src_ref=send.at[target, q],
                    dst_ref=got.at[up, target, q],
                    send_sem=send_sem.at[target, q],
                    recv_sem=recv_sem.at[up, target, q],
                    **where,
                ),
            )

        def start(self):
            for each in self.both:
                each.start()

        def wait_recv(self):
            for each in self.both:
                each.wait_recv()

        def wait_send(self):
            for each in self.both:
                each.wait_send()

    copy = Pair

    strip = min(rows_out, 32)

    def own(c, q, at):
        first = pl.multiple_of((c % splits) * rows_out + at, strip)
        return totals_ref[(c // splits) * nq + q, pl.ds(first, strip)]

    def decode(up, c, q, at, unit):
        coded = got[up, c, q, pl.ds(at, strip), :].astype(jnp.float32)
        root = jnp.exp2(0.125 * jnp.log2(jnp.abs(coded)))
        return jnp.where(coded < 0.0, -root, root) * unit

    def unit_of(up, c, q):
        return got_unit[up, c, q, 0:1, 0:1]

    def code(c, q, parts):
        top = jnp.zeros((8, orbital_count), jnp.float32)
        for at in range(0, rows_out, strip):
            part = parts(at)
            total[pl.ds(at, strip), :] = part
            top = jnp.maximum(top, jnp.max(jnp.abs(part).reshape(-1, 8, orbital_count), axis=0))
        top = jnp.max(jnp.max(top, axis=0, keepdims=True), axis=1, keepdims=True)
        unit = jnp.maximum(top, 1e-30) * 2.0**-15
        send_unit[c, q] = jnp.broadcast_to(unit, (8, LANES))
        inverse = 1.0 / unit
        for at in range(0, rows_out, strip):
            scaled = total[pl.ds(at, strip), :] * inverse
            power = scaled * scaled
            power = power * power
            power = power * power
            send[c, q, pl.ds(at, strip), :] = jnp.where(scaled < 0.0, -power, power).astype(send.dtype)

    @pl.loop(0, (cols - 1) * nq)
    def ends(k):
        i, q = k // nq, k % nq
        for up, target, end in ((1, cols - 1 - i, 0), (0, i, cols - 1)):
            @pl.when(me == end)
            def begin():
                code(target, q, lambda at: own(target, q, at))
                copy(up, target, q).start()

    tiles = (cols - 1) * nq

    @pl.loop(0, tiles + (cols - 1) * LAG)
    def between(k):
        for up in (1, 0):
            turn = k - LAG * (me if up else cols - 1 - me)
            i, q = turn // nq, turn % nq
            target = cols - 1 - i if up else i
            inside = (me > 0) & (me < target) if up else (me < cols - 1) & (me > target)

            @pl.when((turn >= 0) & (turn < tiles) & inside)
            def forward():
                copy(up, target, q).wait_recv()
                unit = unit_of(up, target, q)
                code(target, q, lambda at: own(target, q, at) + decode(up, target, q, at, unit))
                copy(up, target, q).start()

    first_row = (lax.axis_index("row") * cols + me) * rows_out
    mine = first_row // width
    size = jnp.int32(0)
    for b in range(blocks_all):
        size = jnp.where(slot_ref[b] == mine, sizes_ref[b], size)
    vertical = lax.broadcasted_iota(jnp.int32, (strip, 1), 0) + lax.rem(first_row, width)

    total[...] = jnp.zeros(total.shape, jnp.float32)

    @pl.loop(0, nq)
    def finish(q):
        for up, side in ((1, sides[0]), (0, sides[1])):
            @pl.when(side)
            def arrived():
                copy(up, me, q).wait_recv()
                unit = unit_of(up, me, q)
                for at in range(0, rows_out, strip):
                    if up:
                        before = own(me, q, at)
                    else:
                        before = jnp.where(sides[0], total[pl.ds(at, strip), :], own(me, q, at))
                    total[pl.ds(at, strip), :] = before + decode(up, me, q, at, unit)
        for at in range(0, rows_out, strip):
            kept = jnp.where(vertical + at < size, total[pl.ds(at, strip), :], 0.0)
            out_ref[q, pl.ds(at, strip), :] = kept.astype(out_ref.dtype)

    @pl.loop(0, cols * nq)
    def drain(k):
        @pl.when(me != k // nq)
        def sent():
            copy(1, k // nq, k % nq).wait_send()


def on_device(screen, values, sizes, slot, orbitals):
    rows = lax.axis_size("row")
    cols = lax.axis_size("col")
    blocks_all = sizes.shape[0]
    listed, width = values.shape[:2]
    orbital_count = orbitals.shape[1]
    per_row = blocks_all // rows
    per_col = blocks_all // cols
    capacity = max(4, -(-listed // rows))
    seats = rows * capacity
    smem = pl.BlockSpec(memory_space=pltpu.SMEM)
    vmem = pl.BlockSpec(memory_space=pltpu.VMEM)
    dma = pltpu.SemaphoreType.DMA

    order, labels = pl.pallas_call(
        functools.partial(order_kernel, rows, capacity, per_row, per_col),
        out_shape=[jax.ShapeDtypeStruct((seats,), jnp.int32)] * 2,
        in_specs=[smem] * 2,
        out_specs=[smem] * 2,
        scratch_shapes=[pltpu.SMEM((rows,), jnp.int32)],
        name="order_blocks",
    )(screen, slot)

    got, got_labels = pl.pallas_call(
        functools.partial(exchange_kernel, rows, capacity),
        out_shape=[
            jax.ShapeDtypeStruct((seats, width, width), values.dtype),
            jax.ShapeDtypeStruct((rows, 1, LANES), jnp.int32),
        ],
        in_specs=[smem, smem, vmem],
        out_specs=[vmem] * 2,
        scratch_shapes=[
            pltpu.VMEM((rows - 1, capacity, width, width), values.dtype),
            pltpu.VMEM((rows - 1, 1, LANES), jnp.int32),
            dma((rows - 1,)), dma((rows - 1,)), dma((rows - 1,)), dma((rows - 1,)),
        ],
        compiler_params=pltpu.CompilerParams(
            collective_id=0, has_side_effects=True, vmem_limit_bytes=VMEM_LIMIT
        ),
        name="exchange_blocks",
    )(order, labels, values)

    rows_out = per_row * width // cols
    totals = pl.pallas_call(
        functools.partial(contract_kernel, capacity, per_col),
        out_shape=jax.ShapeDtypeStruct((per_row * NQ, width, orbital_count), jnp.float32),
        in_specs=[smem, smem, vmem, vmem],
        out_specs=vmem,
        scratch_shapes=[pltpu.VMEM((per_col, width, orbital_count), orbitals.dtype)],
        compiler_params=pltpu.CompilerParams(vmem_limit_bytes=VMEM_LIMIT),
        name="contract_blocks",
    )(got_labels, sizes, got, orbitals)

    summed = pl.pallas_call(
        functools.partial(scatter_kernel, cols, blocks_all),
        out_shape=jax.ShapeDtypeStruct((NQ, rows_out, orbital_count), jnp.bfloat16),
        in_specs=[smem, smem, vmem],
        out_specs=vmem,
        scratch_shapes=[
            pltpu.VMEM((cols, NQ, rows_out, orbital_count), jnp.bfloat16),
            pltpu.VMEM((2, cols, NQ, rows_out, orbital_count), jnp.bfloat16),
            pltpu.VMEM((cols, NQ, 8, LANES), jnp.float32),
            pltpu.VMEM((2, cols, NQ, 8, LANES), jnp.float32),
            pltpu.VMEM((rows_out, orbital_count), jnp.float32),
            dma((cols, NQ)), dma((2, cols, NQ)), dma((cols, NQ)), dma((2, cols, NQ)),
        ],
        compiler_params=pltpu.CompilerParams(
            collective_id=1, has_side_effects=True, vmem_limit_bytes=VMEM_LIMIT
        ),
        name="scatter_sums",
    )(slot, sizes, totals)
    return summed.transpose(1, 0, 2)


def solution(mesh):
    in_specs = (P(("row", "col"), None), P(("row", "col"), None, None), P(), P(), P("col", None))
    out_specs = P(("row", "col"), None, None)
    return jax.shard_map(
        on_device, mesh=mesh, in_specs=in_specs, out_specs=out_specs, check_vma=False
    )
```

```python
import functools

import jax
import jax.numpy as jnp
from jax import lax
from jax.experimental import pallas as pl
from jax.experimental.pallas import tpu as pltpu
from jax.sharding import PartitionSpec as P

NQ = 4
LANES = 128
LAG = 2
VMEM_LIMIT = 20 * 1024 * 1024


def order_kernel(rows, capacity, per_row, per_col, screen_ref, slot_ref, order_ref, label_ref, count):
    listed = screen_ref.shape[0]

    @pl.loop(0, rows)
    def clear(r):
        count[r] = 0

    @pl.loop(0, rows * capacity, unroll=8)
    def empty(k):
        order_ref[k] = 0
        label_ref[k] = -1

    @pl.loop(0, listed, unroll=8)
    def place(k):
        placed = slot_ref[screen_ref[k, 0]]
        owner = placed // per_row
        seat = owner * capacity + count[owner]
        count[owner] = count[owner] + 1
        order_ref[seat] = k
        out_block = (placed % per_row) * NQ + screen_ref[k, 2]
        label_ref[seat] = out_block * per_col + screen_ref[k, 1] % per_col


def exchange_kernel(
    rows, capacity, order_ref, label_ref, values_ref, got_ref, got_label_ref,
    send, send_label, send_sem, recv_sem, send_label_sem, recv_label_sem,
):
    me = lax.axis_index("row")
    barrier = pltpu.get_barrier_semaphore()
    for step in range(1, rows):
        pl.semaphore_signal(
            barrier, inc=1, device_id={"row": lax.rem(me + step, rows)},
            device_id_type=pl.DeviceIdType.MESH,
        )
    lane = lax.broadcasted_iota(jnp.int32, (1, LANES), 1)

    def fill_label(row):
        line = jnp.full((1, LANES), -1, jnp.int32)
        for j in range(capacity):
            line = jnp.where(lane == j, label_ref[row * capacity + j], line)
        return line

    def copies(step):
        target = lax.rem(me + step, rows)
        return (
            pltpu.make_async_remote_copy(
                src_ref=send.at[step - 1],
                dst_ref=got_ref.at[pl.ds(step * capacity, capacity)],
                send_sem=send_sem.at[step - 1],
                recv_sem=recv_sem.at[step - 1],
                device_id={"row": target},
                device_id_type=pl.DeviceIdType.MESH,
            ),
            pltpu.make_async_remote_copy(
                src_ref=send_label.at[step - 1],
                dst_ref=got_label_ref.at[step],
                send_sem=send_label_sem.at[step - 1],
                recv_sem=recv_label_sem.at[step - 1],
                device_id={"row": target},
                device_id_type=pl.DeviceIdType.MESH,
            ),
        )

    for step in range(1, rows):
        target = lax.rem(me + step, rows)
        for j in range(capacity):
            send[step - 1, j] = values_ref[order_ref[target * capacity + j]]
        send_label[step - 1] = fill_label(target)
    pl.semaphore_wait(barrier, rows - 1)
    for step in range(1, rows):
        for copy in copies(step):
            copy.start()
    for j in range(capacity):
        got_ref[j] = values_ref[order_ref[me * capacity + j]]
    got_label_ref[0] = fill_label(me)
    for step in range(1, rows):
        for copy in copies(step):
            copy.wait()


def contract_kernel(
    capacity, per_col, label_ref, sizes_ref, got_ref, orbitals_ref, totals_ref, coeffs
):
    width = got_ref.shape[1]
    col = lax.axis_index("col")
    vertical = lax.broadcasted_iota(jnp.int32, (width, 1), 0)
    for b in range(per_col):
        size = sizes_ref[col * per_col + b]
        block = orbitals_ref[pl.ds(b * width, width), :].astype(jnp.float32)
        coeffs[b] = jnp.where(vertical < size, block, 0.0).astype(coeffs.dtype)

    @pl.loop(0, totals_ref.shape[0])
    def clear(t):
        totals_ref[t] = jnp.zeros(totals_ref.shape[1:], jnp.float32)

    group = 8

    @pl.loop(0, got_ref.shape[0] // group)
    def add(g):
        places = [g * group + j for j in range(group)]
        labels = [label_ref[k // capacity, 0, k % capacity] for k in places]
        products = [
            jnp.dot(
                got_ref[k], coeffs[jnp.maximum(label, 0) % per_col],
                preferred_element_type=jnp.float32,
            )
            for k, label in zip(places, labels)
        ]
        for label, product in zip(labels, products):
            @pl.when(label >= 0)
            def listed():
                totals_ref[label // per_col] += product


def scatter_kernel(
    cols, blocks_all, slot_ref, sizes_ref, totals_ref, out_ref, send, got, send_unit, got_unit, total,
    send_sem, recv_sem, send_unit_sem, recv_unit_sem,
):
    me = lax.axis_index("col")
    nq, rows_out, orbital_count = out_ref.shape
    width = totals_ref.shape[1]
    splits = width // rows_out
    sides = (me > 0, me < cols - 1)
    barrier = pltpu.get_barrier_semaphore()
    for step in range(1, cols):
        pl.semaphore_signal(
            barrier, inc=1, device_id={"col": lax.rem(me + step, cols)},
            device_id_type=pl.DeviceIdType.MESH,
        )
    pl.semaphore_wait(barrier, cols - 1)

    class Pair:
        def __init__(self, up, target, q):
            where = dict(
                device_id={"col": me + 1 if up else me - 1}, device_id_type=pl.DeviceIdType.MESH
            )
            self.both = (
                pltpu.make_async_remote_copy(
                    src_ref=send_unit.at[target, q],
                    dst_ref=got_unit.at[up, target, q],
                    send_sem=send_unit_sem.at[target, q],
                    recv_sem=recv_unit_sem.at[up, target, q],
                    **where,
                ),
                pltpu.make_async_remote_copy(
                    src_ref=send.at[target, q],
                    dst_ref=got.at[up, target, q],
                    send_sem=send_sem.at[target, q],
                    recv_sem=recv_sem.at[up, target, q],
                    **where,
                ),
            )

        def start(self):
            for each in self.both:
                each.start()

        def wait_recv(self):
            for each in self.both:
                each.wait_recv()

        def wait_send(self):
            for each in self.both:
                each.wait_send()

    copy = Pair

    strip = min(rows_out, 32)

    def own(c, q, at):
        first = pl.multiple_of((c % splits) * rows_out + at, strip)
        return totals_ref[(c // splits) * nq + q, pl.ds(first, strip)]

    def decode(up, c, q, at, unit):
        coded = got[up, c, q, pl.ds(at, strip), :].astype(jnp.float32)
        root = jnp.exp2(0.125 * jnp.log2(jnp.abs(coded)))
        return jnp.where(coded < 0.0, -root, root) * unit

    def unit_of(up, c, q):
        return got_unit[up, c, q, 0:1, 0:1]

    def code(c, q, parts):
        top = jnp.zeros((8, orbital_count), jnp.float32)
        for at in range(0, rows_out, strip):
            part = parts(at)
            total[pl.ds(at, strip), :] = part
            top = jnp.maximum(top, jnp.max(jnp.abs(part).reshape(-1, 8, orbital_count), axis=0))
        top = jnp.max(jnp.max(top, axis=0, keepdims=True), axis=1, keepdims=True)
        unit = jnp.maximum(top, 1e-30) * 2.0**-15
        send_unit[c, q] = jnp.broadcast_to(unit, (8, LANES))
        inverse = 1.0 / unit
        for at in range(0, rows_out, strip):
            scaled = total[pl.ds(at, strip), :] * inverse
            power = scaled * scaled
            power = power * power
            power = power * power
            send[c, q, pl.ds(at, strip), :] = jnp.where(scaled < 0.0, -power, power).astype(send.dtype)

    @pl.loop(0, (cols - 1) * nq)
    def ends(k):
        i, q = k // nq, k % nq
        for up, target, end in ((1, cols - 1 - i, 0), (0, i, cols - 1)):
            @pl.when(me == end)
            def begin():
                code(target, q, lambda at: own(target, q, at))
                copy(up, target, q).start()

    tiles = (cols - 1) * nq

    @pl.loop(0, tiles + (cols - 1) * LAG)
    def between(k):
        for up in (1, 0):
            turn = k - LAG * (me if up else cols - 1 - me)
            i, q = turn // nq, turn % nq
            target = cols - 1 - i if up else i
            inside = (me > 0) & (me < target) if up else (me < cols - 1) & (me > target)

            @pl.when((turn >= 0) & (turn < tiles) & inside)
            def forward():
                copy(up, target, q).wait_recv()
                unit = unit_of(up, target, q)
                code(target, q, lambda at: own(target, q, at) + decode(up, target, q, at, unit))
                copy(up, target, q).start()

    first_row = (lax.axis_index("row") * cols + me) * rows_out
    mine = first_row // width
    size = jnp.int32(0)
    for b in range(blocks_all):
        size = jnp.where(slot_ref[b] == mine, sizes_ref[b], size)
    vertical = lax.broadcasted_iota(jnp.int32, (strip, 1), 0) + lax.rem(first_row, width)

    total[...] = jnp.zeros(total.shape, jnp.float32)

    @pl.loop(0, nq)
    def finish(q):
        for up, side in ((1, sides[0]), (0, sides[1])):
            @pl.when(side)
            def arrived():
                copy(up, me, q).wait_recv()
                unit = unit_of(up, me, q)
                for at in range(0, rows_out, strip):
                    if up:
                        before = own(me, q, at)
                    else:
                        before = jnp.where(sides[0], total[pl.ds(at, strip), :], own(me, q, at))
                    total[pl.ds(at, strip), :] = before + decode(up, me, q, at, unit)
        for at in range(0, rows_out, strip):
            kept = jnp.where(vertical + at < size, total[pl.ds(at, strip), :], 0.0)
            out_ref[q, pl.ds(at, strip), :] = kept.astype(out_ref.dtype)

    @pl.loop(0, cols * nq)
    def drain(k):
        @pl.when(me != k // nq)
        def sent():
            copy(1, k // nq, k % nq).wait_send()


def on_device(screen, values, sizes, slot, orbitals):
    rows = lax.axis_size("row")
    cols = lax.axis_size("col")
    blocks_all = sizes.shape[0]
    listed, width = values.shape[:2]
    orbital_count = orbitals.shape[1]
    per_row = blocks_all // rows
    per_col = blocks_all // cols
    capacity = max(4, -(-listed // rows))
    seats = rows * capacity
    smem = pl.BlockSpec(memory_space=pltpu.SMEM)
    vmem = pl.BlockSpec(memory_space=pltpu.VMEM)
    dma = pltpu.SemaphoreType.DMA

    order, labels = pl.pallas_call(
        functools.partial(order_kernel, rows, capacity, per_row, per_col),
        out_shape=[jax.ShapeDtypeStruct((seats,), jnp.int32)] * 2,
        in_specs=[smem] * 2,
        out_specs=[smem] * 2,
        scratch_shapes=[pltpu.SMEM((rows,), jnp.int32)],
        name="order_blocks",
    )(screen, slot)

    got, got_labels = pl.pallas_call(
        functools.partial(exchange_kernel, rows, capacity),
        out_shape=[
            jax.ShapeDtypeStruct((seats, width, width), values.dtype),
            jax.ShapeDtypeStruct((rows, 1, LANES), jnp.int32),
        ],
        in_specs=[smem, smem, vmem],
        out_specs=[vmem] * 2,
        scratch_shapes=[
            pltpu.VMEM((rows - 1, capacity, width, width), values.dtype),
            pltpu.VMEM((rows - 1, 1, LANES), jnp.int32),
            dma((rows - 1,)), dma((rows - 1,)), dma((rows - 1,)), dma((rows - 1,)),
        ],
        compiler_params=pltpu.CompilerParams(
            collective_id=0, has_side_effects=True, vmem_limit_bytes=VMEM_LIMIT
        ),
        name="exchange_blocks",
    )(order, labels, values)

    rows_out = per_row * width // cols
    totals = pl.pallas_call(
        functools.partial(contract_kernel, capacity, per_col),
        out_shape=jax.ShapeDtypeStruct((per_row * NQ, width, orbital_count), jnp.float32),
        in_specs=[smem, smem, vmem, vmem],
        out_specs=vmem,
        scratch_shapes=[pltpu.VMEM((per_col, width, orbital_count), orbitals.dtype)],
        compiler_params=pltpu.CompilerParams(vmem_limit_bytes=VMEM_LIMIT),
        name="contract_blocks",
    )(got_labels, sizes, got, orbitals)

    summed = pl.pallas_call(
        functools.partial(scatter_kernel, cols, blocks_all),
        out_shape=jax.ShapeDtypeStruct((NQ, rows_out, orbital_count), jnp.bfloat16),
        in_specs=[smem, smem, vmem],
        out_specs=vmem,
        scratch_shapes=[
            pltpu.VMEM((cols, NQ, rows_out, orbital_count), jnp.bfloat16),
            pltpu.VMEM((2, cols, NQ, rows_out, orbital_count), jnp.bfloat16),
            pltpu.VMEM((cols, NQ, 8, LANES), jnp.float32),
            pltpu.VMEM((2, cols, NQ, 8, LANES), jnp.float32),
            pltpu.VMEM((rows_out, orbital_count), jnp.float32),
            dma((cols, NQ)), dma((2, cols, NQ)), dma((cols, NQ)), dma((2, cols, NQ)),
        ],
        compiler_params=pltpu.CompilerParams(
            collective_id=1, has_side_effects=True, vmem_limit_bytes=VMEM_LIMIT
        ),
        name="scatter_sums",
    )(slot, sizes, totals)
    return summed.transpose(1, 0, 2)


def solution(mesh):
    in_specs = (P(("row", "col"), None), P(("row", "col"), None, None), P(), P(), P("col", None))
    out_specs = P(("row", "col"), None, None)
    return jax.shard_map(
        on_device, mesh=mesh, in_specs=in_specs, out_specs=out_specs, check_vma=False
    )
```
